128 devices in a mesh: kgrp: 4 (over z_hi, core), band: 32 (over x, z_lo, y).
Axes of the slice: x: 4, y: 4, z: 4 (z_hi: 2, z_lo: 2; z = z_hi * 2 + z_lo), core: 2. Of those that a mesh axis runs over, the one named last changes fastest.
Arguments:
- densities: bfloat16 [8, 128, 128, 4096], P('kgrp', 'band'), may hold values from -6 to 6
- amplitudes: bfloat16 [8, 8, 128, 128], P('kgrp'), may hold values from -0.046875 to 0.046875
- partner: int32 [8], replicated, may hold values from 0 to 7, as said below
- qtable: int32 [8], replicated, may hold values from 0 to 63
- grid_map: int32 [64, 4096], replicated, may hold values from 0 to 4095, each once within a row
- coulomb: float32 [64, 4096], replicated, may hold values from 0.5 to 2
Outputs:
- ladder: bfloat16 [128, 8, 8, 128], P('band', 'kgrp')
The draws below stay inside these ranges and needn't reach their ends.
Inputs may be any that keep to these rules, and one draw needn't show every extreme that they name: partner is a permutation of the 8 k-pairs; k-pair r lies in group r // 2. The two pairs of a group have their partners in two different groups, neither of them the group itself, and the two pairs whose partners lie in one group belong to two different groups. `grid_map`: each row is a permutation of the 4096 grid positions.
All inputs are finite; a program needn't handle non-finite values.
Results may differ from the reference program's by a relative error of at most 0.0064.
Values may be sent and summed in bfloat16 or wider, within the bound.
No kernel may reach another device: no remote copies, remote signals or barrier semaphores. Data moves between devices by JAX's collectives and lax.ppermute only.
A program may use at most 192 MiB of HBM per device.

```python
import math
import jax
import jax.numpy as jnp
from jax import lax

VB = 128
G = 4096
NQ = 64
IJ = 8
NK = 8


def draw_partner(key, part):
    groups = NK // 2
    first_shift = jax.random.randint(jax.random.fold_in(key, 21), (), 1, groups)
    offset = jax.random.randint(jax.random.fold_in(key, 22), (), 0, groups - 2)
    second_shift = (first_shift + offset) % (groups - 1) + 1
    sender_bit = jax.random.randint(jax.random.fold_in(key, 23), (groups,), 0, 2)
    receiver_bit = jax.random.randint(jax.random.fold_in(key, 24), (groups,), 0, 2)
    group_ids = jnp.arange(groups, dtype=jnp.int32)
    first_dest = (group_ids + first_shift) % groups
    second_dest = (group_ids + second_shift) % groups
    first_target = 2 * first_dest + receiver_bit[first_dest]
    second_target = 2 * second_dest + 1 - receiver_bit[second_dest]
    slot_zero = jnp.where(sender_bit == 0, first_target, second_target)
    slot_one = jnp.where(sender_bit == 0, second_target, first_target)
    return jnp.stack([slot_zero, slot_one], axis=1).reshape(NK).astype(jnp.int32)


def with_ends(entries, key, low, largest):
    place = [jax.random.randint(jax.random.fold_in(key, axis), (), 0, length) for axis, length in enumerate(entries.shape)]
    main_axis = entries.shape.index(max(entries.shape))
    beside = place[:main_axis] + [(place[main_axis] + 1) % entries.shape[main_axis]] + place[main_axis + 1:]
    return entries.at[tuple(place)].set(low).at[tuple(beside)].set(largest)


def spiked(entries, own_key, source, target, blocks, factor):
    owner, partner = [(jnp.arange(entries.shape[axis_at]) // (entries.shape[axis_at] // blocks)).reshape([-1 if axis == axis_at else 1 for axis in range(entries.ndim)]) for axis_at in (source, target)]
    chosen = jax.random.permutation(own_key, blocks)[partner]
    strong = (owner == chosen) | (owner == (partner + blocks // 2) % blocks)
    return jnp.where(strong, factor * entries, entries)


def block_levels(stream_key, extent, shards, least, top_value):
    def one(axis_at, blocks):
        draws = jax.random.uniform(jax.random.fold_in(jax.random.fold_in(stream_key, 6), axis_at), (blocks,), jnp.float32, least / len(shards), top_value / len(shards))
        return jnp.repeat(jnp.exp(draws), extent[axis_at] // blocks).reshape((-1,) + (1,) * (len(extent) - axis_at - 1))

    gain = one(*shards[0])
    for cut in shards[1:]:
        gain = gain * one(*cut)
    return gain


def normal_values(stream_key, shape, spread, bound, shards=(), kind=jnp.bfloat16):
    loudness = block_levels(stream_key, shape, shards, -0.22, 0.18) if shards else 1.0
    drawn = jax.random.normal(stream_key, shape, jnp.float32) * spread * loudness
    return jnp.minimum(jnp.maximum(drawn, -bound), bound).astype(kind)


def bell_draw_with(stream_key, extent, scale, reach, cuts, heavy, held_as=jnp.bfloat16):
    array = scale * jax.random.normal(stream_key, extent, jnp.float32)
    if cuts:
        array = array * block_levels(stream_key, extent, cuts, -0.22, 0.18)
    return jnp.clip(spiked(array, jax.random.fold_in(stream_key, 3), *heavy), -reach, reach).astype(held_as)


def setup_inputs(seed: int = 0) -> dict:
    arg_keys = jax.random.split(jax.random.key(seed), 7)
    return {
        "densities": bell_draw_with(arg_keys[0], (NK, VB, VB, G), 1.0, 6.0, ((0, 4), (1, 32)), (3, 1, 32, 2.75)),
        "amplitudes": normal_values(arg_keys[1], (NK, IJ, VB, VB), (VB * VB) ** -0.5, 0.046875, ((0, 4),)),
        "partner": draw_partner(jax.random.fold_in(arg_keys[6], 71), 0),
        "qtable": with_ends(jax.random.randint(arg_keys[3], (NK,), 0, NQ), jax.random.fold_in(arg_keys[3], 1), 0, NQ - 1).astype(jnp.int32),
        "grid_map": jax.vmap(lambda own: jax.random.permutation(own, G))(jax.random.split(arg_keys[4], NQ)).reshape((NQ, G)).astype(jnp.int32),
        "coulomb": jnp.clip(jnp.exp(jax.random.uniform(arg_keys[5], (NQ, G), jnp.float32, math.log(0.5), math.log(2.0))), 0.5, 2.0),
    }


def make_vertex(densities, qtable, grid_map, coulomb, pair_index):
    transfer = qtable[pair_index]
    grid_rows = grid_map[transfer]
    factors = coulomb[transfer]
    picked = jnp.take(densities[pair_index], grid_rows, axis=2)
    return (picked.astype(jnp.float32) * factors[None, None, :]).astype(jnp.bfloat16)

def reference(densities, amplitudes, partner, qtable, grid_map, coulomb):

    def per_pair(pair_index):
        left_block = make_vertex(densities, qtable, grid_map, coulomb, pair_index)
        right_block = make_vertex(densities, qtable, grid_map, coulomb, partner[pair_index])
        left_wide = left_block.astype(jnp.float32)
        right_wide = right_block.astype(jnp.float32)

        def per_slab(amp_pair):
            mixed = jnp.einsum('acg,cd->adg', left_wide, amp_pair.astype(jnp.float32)).astype(jnp.bfloat16)
            return jnp.einsum('adg,bdg->ab', mixed.astype(jnp.float32), right_wide)
        return lax.map(per_slab, amplitudes[pair_index])
    sums = lax.map(per_pair, jnp.arange(NK, dtype=jnp.int32))
    scaled = sums * (1.0 / math.sqrt(G))
    return jnp.transpose(scaled, (2, 0, 1, 3)).astype(jnp.bfloat16)
```

```python
import functools
import math

import jax
import jax.numpy as jnp
from jax import lax
from jax.experimental import pallas as pl
from jax.experimental.pallas import tpu as pltpu
from jax.sharding import PartitionSpec as P

G = 4096
AXES = ("kgrp", "band")
CHUNKS = 4
GC = 32 // CHUNKS
BLOCK = 512
BF, F32 = jnp.bfloat16, jnp.float32


def column(row):
    return jnp.transpose(jnp.broadcast_to(row, (128, 128)), (1, 0))


def gather_kernel(map_ref, coul_ref, dens_ref, out_ref, onehot):
    lane = lax.broadcasted_iota(jnp.int32, (128, 128), 1)
    for b in range(BLOCK // 128):
        col = column(map_ref[0, 0, b : b + 1, :])
        high = (col >> 7).astype(F32).astype(BF)
        low = jnp.where((col & 127) == lane, 1.0, 0.0).astype(BF)
        zero = jnp.zeros_like(low)
        for kb in range(G // 128):
            onehot[b * 128 : (b + 1) * 128, kb * 128 : (kb + 1) * 128] = jnp.where(
                high == jnp.asarray(kb, BF), low, zero
            )
    picked = lax.dot_general(
        onehot[...], dens_ref[0], (((1,), (1,)), ((), ())), preferred_element_type=F32
    )
    n = 128 // GC
    for b in range(BLOCK // 128):
        factor = column(coul_ref[0, 0, b : b + 1, :])
        for l in range(4):
            scaled = picked[b * 128 : (b + 1) * 128, l * 128 : (l + 1) * 128] * factor
            out_ref[b * n : (b + 1) * n, 0, :, l * 128 : (l + 1) * 128] = scaled.reshape(n, GC, 128).astype(BF)


def gather(dens, maps, couls):
    steps = 128 * GC // BLOCK
    small = pl.BlockSpec((1, 1, BLOCK // 128, 128), lambda r, i: (r, i, 0, 0))
    return pl.pallas_call(
        gather_kernel,
        grid=(2, steps),
        in_specs=[small, small, pl.BlockSpec((1, 512, G), lambda r, i: (r, 0, 0))],
        out_specs=pl.BlockSpec((BLOCK // GC, 1, GC, 512), lambda r, i: (i, r, 0, 0)),
        out_shape=jax.ShapeDtypeStruct((128, 2, GC, 512), BF),
        scratch_shapes=[pltpu.VMEM((BLOCK, G), BF)],
        compiler_params=pltpu.CompilerParams(vmem_limit_bytes=60 * 2**20),
        cost_estimate=pl.CostEstimate(flops=4 * 128 * GC * G * 512, bytes_accessed=10**7, transcendentals=0),
        name="vertex_rows",
    )(maps.reshape(2, steps, BLOCK // 128, 128), couls.reshape(2, steps, BLOCK // 128, 128), dens)


def ladder_kernel(first, last, partner_ref, recv_ref, amp_ref, *refs):
    refs = list(refs)
    acc_in = None if first else refs.pop(0)
    out_ref, vert, mixed, wide = refs[:4]
    r = pl.program_id(0)

    @pl.when(r == 0)
    def _():
        for k in range(4):
            for r2 in range(2):
                for h in range(GC // 8):
                    for a4 in range(4):
                        wide[a4] = (
                            recv_ref[k, :, r2, h * 8 : (h + 1) * 8, a4 * 128 : (a4 + 1) * 128]
                            .astype(F32)
                            .reshape(256, 128)
                        )
                    for g in range(8):
                        for a4 in range(4):
                            vert[2 * k + r2, h * 8 + g, a4 * 32 : (a4 + 1) * 32, :] = wide[
                                a4, pl.ds(g, 32, stride=8), :
                            ].astype(BF)

    left = vert[r].reshape(GC * 128, 128)
    for p in range(4):
        amp = jnp.concatenate([amp_ref[0, 2 * p], amp_ref[0, 2 * p + 1]], axis=1)
        m = jnp.dot(left, amp, preferred_element_type=F32).astype(BF)
        for i in range(2):
            for g in range(GC):
                mixed[(2 * p + i) * 128 : (2 * p + i + 1) * 128, g * 128 : (g + 1) * 128] = m[
                    g * 128 : (g + 1) * 128, i * 128 : (i + 1) * 128
                ]
    w = vert[partner_ref[r]]
    right = jnp.concatenate([w[g] for g in range(GC)], axis=1)
    res = lax.dot_general(mixed[...], right, (((1,), (1,)), ((), ())), preferred_element_type=F32)
    if not first:
        res = res + acc_in[0]
    if last:
        total = refs[4]
        total[...] = res
        for s in range(32):
            out_ref[0, s, 0, :, :] = total[pl.ds(s, 32, stride=32), :].astype(BF)
    else:
        out_ref[0] = res


def ladder(partner, recv, amp, acc, last):
    ins = [
        pl.BlockSpec((4, 32, 2, GC, 512), lambda r, p: (0, 0, 0, 0, 0)),
        pl.BlockSpec((1, 8, 128, 128), lambda r, p: (r, 0, 0, 0)),
    ]
    args = [partner, recv.reshape(4, 32, 2, GC, 512), amp]
    if acc is not None:
        ins.append(pl.BlockSpec((1, 1024, 128), lambda r, p: (r, 0, 0)))
        args.append(acc)
    scratch = [
        pltpu.VMEM((8, GC, 128, 128), BF),
        pltpu.VMEM((1024, GC * 128), BF),
        pltpu.VMEM((4, 256, 128), F32),
    ]
    if last:
        out_spec = pl.BlockSpec((1, 32, 1, 32, 128), lambda r, p: (r // 2, 0, r % 2, 0, 0))
        out_shape = jax.ShapeDtypeStruct((4, 32, 2, 32, 128), BF)
        scratch.append(pltpu.VMEM((1024, 128), F32))
    else:
        out_spec = pl.BlockSpec((1, 1024, 128), lambda r, p: (r, 0, 0))
        out_shape = jax.ShapeDtypeStruct((8, 1024, 128), F32)
    return pl.pallas_call(
        functools.partial(ladder_kernel, acc is None, last),
        grid_spec=pltpu.PrefetchScalarGridSpec(
            num_scalar_prefetch=1, grid=(8,), in_specs=ins, out_specs=out_spec, scratch_shapes=scratch
        ),
        out_shape=out_shape,
        compiler_params=pltpu.CompilerParams(vmem_limit_bytes=60 * 2**20),
        cost_estimate=pl.CostEstimate(flops=32 * 8 * 128**3 * GC // 8 * 8, bytes_accessed=12 * 10**6, transcendentals=0),
        name="ladder_sum",
    )(*args)


def shards(densities, amplitudes, partner, qtable, grid_map, coulomb):
    own = lax.axis_index("kgrp") * 2
    amp = lax.all_gather(amplitudes, "kgrp", axis=0, tiled=True)
    rows = [qtable[own + i] for i in range(2)]
    maps = jnp.concatenate([lax.dynamic_slice_in_dim(grid_map, q, 1, 0) for q in rows], axis=0)
    couls = jnp.concatenate([lax.dynamic_slice_in_dim(coulomb, q, 1, 0) for q in rows], axis=0)
    dens = densities.reshape(2, 512, G)
    width = 128 * GC
    received = []
    for q in range(CHUNKS):
        part = slice(q * width, (q + 1) * width)
        sent = gather(dens, maps[:, part], couls[:, part])
        received.append(lax.all_to_all(sent, AXES, 0, 0, tiled=True))
    acc = None
    for q in range(CHUNKS):
        acc = ladder(partner, received[q], amp, acc, q == CHUNKS - 1)
    parts = lax.all_to_all(acc.reshape(128, 64, 128), AXES, 0, 0, tiled=True)
    total = jnp.sum(parts.astype(F32), axis=0) * (1.0 / math.sqrt(G))
    total = total.astype(BF).reshape(2, 8, 4, 4, 32)
    return jnp.transpose(total, (2, 0, 1, 4, 3)).reshape(4, 2, 8, 128)


def solution(mesh):
    in_specs = (P("kgrp", "band", None, None), P("kgrp", None, None, None), P(), P(), P(), P())
    out_specs = P("band", "kgrp", None, None)
    return jax.shard_map(shards, mesh=mesh, in_specs=in_specs, out_specs=out_specs, check_vma=False)
```

```python
import functools
import math

import jax
import jax.numpy as jnp
from jax import lax
from jax.experimental import pallas as pl
from jax.experimental.pallas import tpu as pltpu
from jax.sharding import PartitionSpec as P

G = 4096
AXES = ("kgrp", "band")
CHUNKS = 2
GC = 32 // CHUNKS
BLOCK = 512
BF, F32 = jnp.bfloat16, jnp.float32


def column(row):
    return jnp.transpose(jnp.broadcast_to(row, (128, 128)), (1, 0))


def pick(rows, row):
    here = lax.broadcasted_iota(jnp.int32, rows.shape, 0) == row
    return jnp.sum(jnp.where(here, rows, jnp.zeros_like(rows)), axis=0, keepdims=True)


def gather_kernel(own_ref, qtable_ref, map_ref, coul_ref, dens_ref, out_ref, onehot):
    row = lax.rem(qtable_ref[own_ref[0] + pl.program_id(0)], 8)
    lane = lax.broadcasted_iota(jnp.int32, (128, 128), 1)
    for b in range(BLOCK // 128):
        col = column(pick(map_ref[:, b * 128 : (b + 1) * 128], row))
        high = (col >> 7).astype(F32).astype(BF)
        low = jnp.where((col & 127) == lane, 1.0, 0.0).astype(BF)
        zero = jnp.zeros_like(low)
        for kb in range(G // 128):
            onehot[b * 128 : (b + 1) * 128, kb * 128 : (kb + 1) * 128] = jnp.where(
                high == jnp.asarray(kb, BF), low, zero
            )
    picked = lax.dot_general(
        onehot[...], dens_ref[0], (((1,), (1,)), ((), ())), preferred_element_type=F32
    )
    n = 128 // GC
    for b in range(BLOCK // 128):
        factor = column(pick(coul_ref[:, b * 128 : (b + 1) * 128], row))
        for l in range(4):
            scaled = picked[b * 128 : (b + 1) * 128, l * 128 : (l + 1) * 128] * factor
            out_ref[b * n : (b + 1) * n, 0, :, l * 128 : (l + 1) * 128] = scaled.reshape(n, GC, 128).astype(BF)


def gather(own, qtable, grid_map, coulomb, dens, chunk):
    steps = 128 * GC // BLOCK
    table = pl.BlockSpec((8, BLOCK), lambda r, i, own, qt: (qt[own[0] + r] // 8, chunk * steps + i))
    return pl.pallas_call(
        gather_kernel,
        grid_spec=pltpu.PrefetchScalarGridSpec(
            num_scalar_prefetch=2,
            grid=(2, steps),
            in_specs=[table, table, pl.BlockSpec((1, 512, G), lambda r, i, own, qt: (r, 0, 0))],
            out_specs=pl.BlockSpec((BLOCK // GC, 1, GC, 512), lambda r, i, own, qt: (i, r, 0, 0)),
            scratch_shapes=[pltpu.VMEM((BLOCK, G), BF)],
        ),
        out_shape=jax.ShapeDtypeStruct((128, 2, GC, 512), BF),
        compiler_params=pltpu.CompilerParams(vmem_limit_bytes=60 * 2**20),
        cost_estimate=pl.CostEstimate(flops=4 * 128 * GC * G * 512, bytes_accessed=10**7, transcendentals=0),
        name="vertex_rows",
    )(own, qtable, grid_map, coulomb, dens)


def ladder_kernel(first, last, own_ref, partner_ref, recv_ref, amp_ref, *refs):
    refs = list(refs)
    acc_in = None if first else refs.pop(0)
    out_ref, vert, mixed, wide = refs[:4]
    r = pl.program_id(0)

    @pl.when(r == 0)
    def _():
        for k in range(4):
            for r2 in range(2):
                for h in range(GC // 8):
                    for a4 in range(4):
                        wide[a4] = (
                            recv_ref[k, :, r2, h * 8 : (h + 1) * 8, a4 * 128 : (a4 + 1) * 128]
                            .astype(F32)
                            .reshape(256, 128)
                        )
                    for g in range(8):
                        for a4 in range(4):
                            vert[2 * k + r2, h * 8 + g, a4 * 32 : (a4 + 1) * 32, :] = wide[
                                a4, pl.ds(g, 32, stride=8), :
                            ].astype(BF)

    amp = jnp.concatenate([amp_ref[0, 0, ij] for ij in range(8)], axis=1)
    for g in range(GC):
        m = jnp.dot(vert[r, g], amp, preferred_element_type=F32).astype(BF)
        for ij in range(8):
            mixed[ij * 128 : (ij + 1) * 128, g * 128 : (g + 1) * 128] = m[:, ij * 128 : (ij + 1) * 128]
    w = vert[partner_ref[r]]
    right = jnp.concatenate([w[g] for g in range(GC)], axis=1)
    res = lax.dot_general(mixed[...], right, (((1,), (1,)), ((), ())), preferred_element_type=F32)
    if not first:
        res = res + acc_in[0]
    if last:
        total = refs[4]
        total[...] = res
        for s in range(32):
            out_ref[0, s, 0, :, :] = total[pl.ds(s, 32, stride=32), :].astype(BF)
    else:
        out_ref[0] = res


def piece(r, own):
    away = (r // 2) ^ (own // 2)
    return (away % 2) * 2 + away // 2


def ladder(own, partner, recv, amp, acc, last):
    ins = [
        pl.BlockSpec((4, 32, 2, GC, 512), lambda r, o, p: (0, 0, 0, 0, 0)),
        pl.BlockSpec((1, 1, 8, 128, 128), lambda r, o, p: (piece(r, o[0]), r % 2, 0, 0, 0)),
    ]
    args = [own, partner, recv.reshape(4, 32, 2, GC, 512), amp]
    if acc is not None:
        ins.append(pl.BlockSpec((1, 1024, 128), lambda r, o, p: (r, 0, 0)))
        args.append(acc)
    scratch = [
        pltpu.VMEM((8, GC, 128, 128), BF),
        pltpu.VMEM((1024, GC * 128), BF),
        pltpu.VMEM((4, 256, 128), F32),
    ]
    if last:
        out_spec = pl.BlockSpec((1, 32, 1, 32, 128), lambda r, o, p: (r // 2, 0, r % 2, 0, 0))
        out_shape = jax.ShapeDtypeStruct((4, 32, 2, 32, 128), BF)
        scratch.append(pltpu.VMEM((1024, 128), F32))
    else:
        out_spec = pl.BlockSpec((1, 1024, 128), lambda r, o, p: (r, 0, 0))
        out_shape = jax.ShapeDtypeStruct((8, 1024, 128), F32)
    return pl.pallas_call(
        functools.partial(ladder_kernel, acc is None, last),
        grid_spec=pltpu.PrefetchScalarGridSpec(
            num_scalar_prefetch=2, grid=(8,), in_specs=ins, out_specs=out_spec, scratch_shapes=scratch
        ),
        out_shape=out_shape,
        compiler_params=pltpu.CompilerParams(vmem_limit_bytes=60 * 2**20),
        cost_estimate=pl.CostEstimate(flops=4 * 64 * 128**3 * GC, bytes_accessed=12 * 10**6, transcendentals=0),
        name="ladder_sum",
    )(*args)


def swap(array, bit):
    return lax.ppermute(array, "kgrp", [(i, i ^ bit) for i in range(4)])


def shards(densities, amplitudes, partner, qtable, grid_map, coulomb):
    own = (lax.axis_index("kgrp") * 2).astype(jnp.int32).reshape(1)
    across = swap(amplitudes, 2)
    dens = densities.reshape(2, 512, G)
    received = []
    for q in range(CHUNKS):
        sent = gather(own, qtable, grid_map, coulomb, dens, q)
        if q == 0:
            sent, across = lax.optimization_barrier((sent, across))
            here = jnp.stack([amplitudes, across])
            amp = jnp.concatenate([here, swap(here, 1)])
        received.append(lax.all_to_all(sent, AXES, 0, 0, tiled=True))
    acc = None
    for q in range(CHUNKS):
        acc = ladder(own, partner, received[q], amp, acc, q == CHUNKS - 1)
    parts = lax.all_to_all(acc.reshape(128, 64, 128), AXES, 0, 0, tiled=True)
    total = jnp.sum(parts.astype(F32), axis=0) * (1.0 / math.sqrt(G))
    total = total.astype(BF).reshape(2, 8, 4, 4, 32)
    return jnp.transpose(total, (2, 0, 1, 4, 3)).reshape(4, 2, 8, 128)


def solution(mesh):
    in_specs = (P("kgrp", "band", None, None), P("kgrp", None, None, None), P(), P(), P(), P())
    out_specs = P("band", "kgrp", None, None)
    return jax.shard_map(shards, mesh=mesh, in_specs=in_specs, out_specs=out_specs, check_vma=False)
```

```python
import functools
import math

import jax
import jax.numpy as jnp
from jax import lax
from jax.experimental import pallas as pl
from jax.experimental.pallas import tpu as pltpu
from jax.sharding import PartitionSpec as P

G = 4096
AXES = ("kgrp", "band")
SIZES = (20, 12)
BF, F32 = jnp.bfloat16, jnp.float32


def pick(rows, row):
    here = lax.broadcasted_iota(jnp.int32, rows.shape, 0) == row
    return jnp.sum(jnp.where(here, rows, jnp.zeros_like(rows)), axis=0, keepdims=True)


def gather_kernel(gc, start, own_ref, qtable_ref, map_ref, dens_ref, out_ref, table, place_v, place_s, sem):
    row = lax.rem(qtable_ref[own_ref[0] + pl.program_id(0)], 8)
    for b in range(gc):
        p = pick(map_ref[:, start + b * 128 : start + (b + 1) * 128], row)
        place_v[b : b + 1, :] = ((p & 1) << 14) + ((p >> 1) << 3)
    copy = pltpu.make_async_copy(place_v, place_s, sem)
    copy.start()
    eye = lax.broadcasted_iota(jnp.int32, (256, 256), 0) == lax.broadcasted_iota(jnp.int32, (256, 256), 1)
    eye = jnp.where(eye, 1.0, 0.0).astype(BF)
    for i in range(G // 256):
        turned = lax.dot_general(
            eye, dens_ref[0, :, i * 256 : (i + 1) * 256], (((1,), (1,)), ((), ())), preferred_element_type=F32
        )
        for a in range(4):
            table[pl.ds(i * 1024 + a, 256, stride=4), :] = turned[:, a * 128 : (a + 1) * 128]
        for j in range(128):
            at = i * 1024 + j * 8
            table[4 * G + at : 4 * G + at + 8, :] = pltpu.roll(table[at : at + 8, :], 4, 0)
    copy.wait()
    low = lax.broadcasted_iota(jnp.int32, (8, 128), 0) < 4
    step = math.lcm(128, gc)

    def body(it, _):
        for quad in range(step // 4):
            pairs = []
            for h in range(2):
                at = quad * 4 + h * 2
                block = it * (step // 128) + at // 128
                first = place_s[block, at % 128]
                second = place_s[block, at % 128 + 1] ^ (1 << 14)
                pairs.append(
                    jnp.where(
                        low,
                        table[pl.ds(pl.multiple_of(first, 8), 8), :],
                        table[pl.ds(pl.multiple_of(second, 8), 8), :],
                    )
                )
            device, w = divmod(quad * 4, gc)
            out_ref[it * (step // gc) + device, 0, 4 * w : 4 * w + 16, :] = jnp.concatenate(pairs, axis=0).astype(BF)
        return 0

    lax.fori_loop(0, 128 * gc // step, body, 0)


def gather(own, qtable, grid_map, dens, gc, start):
    return pl.pallas_call(
        functools.partial(gather_kernel, gc, start),
        grid_spec=pltpu.PrefetchScalarGridSpec(
            num_scalar_prefetch=2,
            grid=(2,),
            in_specs=[
                pl.BlockSpec((8, G), lambda r, own, qt: (qt[own[0] + r] // 8, 0)),
                pl.BlockSpec((1, 512, G), lambda r, own, qt: (r, 0, 0)),
            ],
            out_specs=pl.BlockSpec((128, 1, 4 * gc, 128), lambda r, own, qt: (0, r, 0, 0)),
            scratch_shapes=[
                pltpu.VMEM((8 * G, 128), F32),
                pltpu.VMEM((gc, 128), jnp.int32),
                pltpu.SMEM((gc, 128), jnp.int32),
                pltpu.SemaphoreType.DMA,
            ],
        ),
        out_shape=jax.ShapeDtypeStruct((128, 2, 4 * gc, 128), BF),
        compiler_params=pltpu.CompilerParams(vmem_limit_bytes=60 * 2**20),
        cost_estimate=pl.CostEstimate(flops=2 * 10**10, bytes_accessed=10**7, transcendentals=0),
        name="vertex_rows",
    )(own, qtable, grid_map, dens)


def ladder_kernel(gc, first, last, own_ref, partner_ref, qtable_ref, coul_ref, recv_ref, amp_ref, *refs):
    refs = list(refs)
    acc_in = None if first else refs.pop(0)
    out_ref, vert, mixed, wide = refs[:4]
    k = pl.program_id(0)

    @pl.when(k == 0)
    def _():
        for k in range(4):
            for r2 in range(2):
                part = wide.at[r2]
                for s in range(32):
                    part[s * (4 * gc + 8) : s * (4 * gc + 8) + 4 * gc, :] = recv_ref[k, s, r2].astype(F32)
                base = qtable_ref[2 * k + r2] * gc
                for g in range(gc):
                    factor = coul_ref[base + g]
                    for a4 in range(4):
                        rows = part[pl.ds(4 * g + a4, 32, stride=4 * gc + 8), :]
                        vert[2 * k + r2, g, a4 * 32 : (a4 + 1) * 32, :] = (rows * factor).astype(BF)

    for i in range(2):
        amp = jnp.concatenate([amp_ref[0, i, ij] for ij in range(8)], axis=1)
        for g in range(gc):
            m = jnp.dot(vert[2 * k + i, g], amp, preferred_element_type=F32).astype(BF)
            for ij in range(8):
                mixed[i, ij * 128 : (ij + 1) * 128, g * 128 : (g + 1) * 128] = m[:, ij * 128 : (ij + 1) * 128]
    for i in range(2):
        other = partner_ref[2 * k + i]
        right = jnp.concatenate([vert[other, g] for g in range(gc)], axis=1)
        res = lax.dot_general(mixed[i], right, (((1,), (1,)), ((), ())), preferred_element_type=F32)
        if not first:
            res = res + acc_in[i]
        if last:
            total = refs[4].at[i]
            total[...] = res
            for s in range(32):
                out_ref[0, s, i, :, :] = total[pl.ds(s, 32, stride=32), :].astype(BF)
        else:
            out_ref[i] = res


def piece(k, own):
    away = k ^ (own // 2)
    return (away % 2) * 2 + away // 2


def ladder(own, partner, qtable, coul, recv, amp, acc, last, gc):
    ins = [
        pl.BlockSpec((4, 32, 2, 4 * gc, 128), lambda k, *_: (0, 0, 0, 0, 0)),
        pl.BlockSpec((1, 2, 8, 128, 128), lambda k, o, *_: (piece(k, o[0]), 0, 0, 0, 0)),
    ]
    args = [own, partner, qtable, coul, recv.reshape(4, 32, 2, 4 * gc, 128), amp]
    if acc is not None:
        ins.append(pl.BlockSpec((2, 1024, 128), lambda k, *_: (k, 0, 0)))
        args.append(acc)
    scratch = [
        pltpu.VMEM((8, gc, 128, 128), BF),
        pltpu.VMEM((2, 1024, gc * 128), BF),
        pltpu.VMEM((2, 32 * (4 * gc + 8), 128), F32),
    ]
    if last:
        out_spec = pl.BlockSpec((1, 32, 2, 32, 128), lambda k, *_: (k, 0, 0, 0, 0))
        out_shape = jax.ShapeDtypeStruct((4, 32, 2, 32, 128), BF)
        scratch.append(pltpu.VMEM((2, 1024, 128), F32))
    else:
        out_spec = pl.BlockSpec((2, 1024, 128), lambda k, *_: (k, 0, 0))
        out_shape = jax.ShapeDtypeStruct((8, 1024, 128), F32)
    return pl.pallas_call(
        functools.partial(ladder_kernel, gc, acc is None, last),
        grid_spec=pltpu.PrefetchScalarGridSpec(
            num_scalar_prefetch=4, grid=(4,), in_specs=ins, out_specs=out_spec, scratch_shapes=scratch
        ),
        out_shape=out_shape,
        compiler_params=pltpu.CompilerParams(vmem_limit_bytes=60 * 2**20),
        cost_estimate=pl.CostEstimate(flops=4 * 64 * 128**3 * gc, bytes_accessed=12 * 10**6, transcendentals=0),
        name="ladder_sum",
    )(*args)


def swap(array, bit):
    return lax.ppermute(array, "kgrp", [(i, i ^ bit) for i in range(4)])


def shards(densities, amplitudes, partner, qtable, grid_map, coulomb):
    own = (lax.axis_index("kgrp") * 2).astype(jnp.int32).reshape(1)
    across = swap(amplitudes, 2)
    dens = densities.reshape(2, 512, G)
    device = lax.axis_index(AXES)
    received, couls, start = [], [], 0
    for q, gc in enumerate(SIZES):
        sent = gather(own, qtable, grid_map, dens, gc, start)
        if q == 0:
            sent, across = lax.optimization_barrier((sent, across))
            here = jnp.stack([amplitudes, across])
            amp = jnp.concatenate([here, swap(here, 1)])
        received.append(lax.all_to_all(sent, AXES, 0, 0, tiled=True))
        couls.append(lax.dynamic_slice(coulomb, (0, start + device * gc), (64, gc)).reshape(-1))
        start += 128 * gc
    acc = None
    for q, gc in enumerate(SIZES):
        acc = ladder(own, partner, qtable, couls[q], received[q], amp, acc, q == len(SIZES) - 1, gc)
    parts = lax.all_to_all(acc.reshape(128, 64, 128), AXES, 0, 0, tiled=True)
    total = jnp.sum(parts.astype(F32), axis=0) * (1.0 / math.sqrt(G))
    total = total.astype(BF).reshape(2, 8, 4, 4, 32)
    return jnp.transpose(total, (2, 0, 1, 4, 3)).reshape(4, 2, 8, 128)


def solution(mesh):
    in_specs = (P("kgrp", "band", None, None), P("kgrp", None, None, None), P(), P(), P(), P())
    out_specs = P("band", "kgrp", None, None)
    return jax.shard_map(shards, mesh=mesh, in_specs=in_specs, out_specs=out_specs, check_vma=False)
```

```python
import functools
import math

import jax
import jax.numpy as jnp
from jax import lax
from jax.experimental import pallas as pl
from jax.experimental.pallas import tpu as pltpu
from jax.sharding import Mesh
from jax.sharding import PartitionSpec as P

G = 4096
KGRP = ("zhi", "core")
AXES = KGRP + ("band",)
SIZES = (20, 12)
BF, F32 = jnp.bfloat16, jnp.float32


def pick(rows, row):
    here = lax.broadcasted_iota(jnp.int32, rows.shape, 0) == row
    return jnp.sum(jnp.where(here, rows, jnp.zeros_like(rows)), axis=0, keepdims=True)


def gather_kernel(gc, start, own_ref, qtable_ref, map_ref, dens_ref, out_ref, table, place_v, place_s, sem):
    row = lax.rem(qtable_ref[own_ref[0] + pl.program_id(0)], 8)
    for b in range(gc):
        p = pick(map_ref[:, start + b * 128 : start + (b + 1) * 128], row)
        place_v[b : b + 1, :] = ((p & 1) << 14) + ((p >> 1) << 3)
    copy = pltpu.make_async_copy(place_v, place_s, sem)
    copy.start()
    eye = lax.broadcasted_iota(jnp.int32, (256, 256), 0) == lax.broadcasted_iota(jnp.int32, (256, 256), 1)
    eye = jnp.where(eye, 1.0, 0.0).astype(BF)
    for i in range(G // 256):
        turned = lax.dot_general(
            eye, dens_ref[0, :, i * 256 : (i + 1) * 256], (((1,), (1,)), ((), ())), preferred_element_type=F32
        )
        for a in range(4):
            table[pl.ds(i * 1024 + a, 256, stride=4), :] = turned[:, a * 128 : (a + 1) * 128]
        for j in range(128):
            at = i * 1024 + j * 8
            table[4 * G + at : 4 * G + at + 8, :] = pltpu.roll(table[at : at + 8, :], 4, 0)
    copy.wait()
    low = lax.broadcasted_iota(jnp.int32, (8, 128), 0) < 4
    step = math.lcm(128, gc)

    def body(it, _):
        for quad in range(step // 4):
            pairs = []
            for h in range(2):
                at = quad * 4 + h * 2
                block = it * (step // 128) + at // 128
                first = place_s[block, at % 128]
                second = place_s[block, at % 128 + 1] ^ (1 << 14)
                pairs.append(
                    jnp.where(
                        low,
                        table[pl.ds(pl.multiple_of(first, 8), 8), :],
                        table[pl.ds(pl.multiple_of(second, 8), 8), :],
                    )
                )
            device, w = divmod(quad * 4, gc)
            out_ref[it * (step // gc) + device, 0, 4 * w : 4 * w + 16, :] = jnp.concatenate(pairs, axis=0).astype(BF)
        return 0

    lax.fori_loop(0, 128 * gc // step, body, 0)


def gather(own, qtable, grid_map, dens, gc, start):
    return pl.pallas_call(
        functools.partial(gather_kernel, gc, start),
        grid_spec=pltpu.PrefetchScalarGridSpec(
            num_scalar_prefetch=2,
            grid=(2,),
            in_specs=[
                pl.BlockSpec((8, G), lambda r, own, qt: (qt[own[0] + r] // 8, 0)),
                pl.BlockSpec((1, 512, G), lambda r, own, qt: (r, 0, 0)),
            ],
            out_specs=pl.BlockSpec((128, 1, 4 * gc, 128), lambda r, own, qt: (0, r, 0, 0)),
            scratch_shapes=[
                pltpu.VMEM((8 * G, 128), F32),
                pltpu.VMEM((gc, 128), jnp.int32),
                pltpu.SMEM((gc, 128), jnp.int32),
                pltpu.SemaphoreType.DMA,
            ],
        ),
        out_shape=jax.ShapeDtypeStruct((128, 2, 4 * gc, 128), BF),
        compiler_params=pltpu.CompilerParams(vmem_limit_bytes=60 * 2**20),
        cost_estimate=pl.CostEstimate(flops=2 * 10**10, bytes_accessed=10**7, transcendentals=0),
        name="vertex_rows",
    )(own, qtable, grid_map, dens)


def ladder_kernel(gc, first, last, own_ref, partner_ref, qtable_ref, coul_ref, recv_ref, amp_ref, *refs):
    refs = list(refs)
    acc_in = None if first else refs.pop(0)
    outs = [refs.pop(0) for _ in range(1 + last)]
    vert, mixed, wide = refs[:3]
    t = pl.program_id(0)
    k = turn(t, own_ref[0], last)

    @pl.when(t == 0)
    def _():
        for k in range(4):
            for r2 in range(2):
                part = wide.at[r2]
                for s in range(32):
                    part[s * (4 * gc + 8) : s * (4 * gc + 8) + 4 * gc, :] = recv_ref[k, s, r2].astype(F32)
                q = qtable_ref[2 * k + r2]
                for g in range(gc):
                    factor = coul_ref[q, g]
                    for a4 in range(4):
                        rows = part[pl.ds(4 * g + a4, 32, stride=4 * gc + 8), :]
                        vert[2 * k + r2, g, a4 * 32 : (a4 + 1) * 32, :] = (rows * factor).astype(BF)

    for i in range(2):
        amp = jnp.concatenate([amp_ref[0, i, ij] for ij in range(8)], axis=1)
        for g in range(gc):
            m = jnp.dot(vert[2 * k + i, g], amp, preferred_element_type=F32).astype(BF)
            for ij in range(8):
                mixed[i, ij * 128 : (ij + 1) * 128, g * 128 : (g + 1) * 128] = m[:, ij * 128 : (ij + 1) * 128]
    for i in range(2):
        other = partner_ref[2 * k + i]
        right = jnp.concatenate([vert[other, g] for g in range(gc)], axis=1)
        res = lax.dot_general(mixed[i], right, (((1,), (1,)), ((), ())), preferred_element_type=F32)
        if not first:
            res = res + acc_in[i]
        if last:
            for n in range(32):
                refs[3][i, n * 40 : n * 40 + 32, :] = res[n * 32 : (n + 1) * 32]
        else:
            outs[0][i] = res
    if last:
        for half, out_ref in enumerate(outs):

            @pl.when(t // 2 == half)
            def _():
                for i in range(2):
                    for s in range(32):
                        out_ref[0, s, i, :, :] = refs[3][i, pl.ds(s, 32, stride=40), :].astype(BF)


def turn(t, own, last):
    return 2 * (t % 2) + (((own // 2) % 2) ^ (1 - t // 2)) if last else t


def piece(k, own):
    away = k ^ (own // 2)
    return (away % 2) * 2 + away // 2


def ladder(own, partner, qtable, coul, recv, amp, acc, last, gc):
    ins = [
        pl.BlockSpec((4, 32, 2, 4 * gc, 128), lambda k, *_: (0, 0, 0, 0, 0)),
        pl.BlockSpec((1, 2, 8, 128, 128), lambda t, o, *_: (piece(turn(t, o[0], last), o[0]), 0, 0, 0, 0)),
    ]
    args = [own, partner, qtable, coul, recv.reshape(4, 32, 2, 4 * gc, 128), amp]
    if acc is not None:
        ins.append(pl.BlockSpec((2, 1024, 128), lambda t, o, *_: (turn(t, o[0], last), 0, 0)))
        args.append(acc)
    scratch = [
        pltpu.VMEM((8, gc, 128, 128), BF),
        pltpu.VMEM((2, 1024, gc * 128), BF),
        pltpu.VMEM((2, 33 * (4 * gc + 8), 128), F32),
    ]
    if last:
        out_spec = [
            pl.BlockSpec((1, 32, 2, 32, 128), lambda t, *_: (jnp.minimum(t, 1), 0, 0, 0, 0)),
            pl.BlockSpec((1, 32, 2, 32, 128), lambda t, *_: (jnp.maximum(t - 2, 0), 0, 0, 0, 0)),
        ]
        out_shape = [jax.ShapeDtypeStruct((2, 32, 2, 32, 128), BF)] * 2
        scratch.append(pltpu.VMEM((2, 33 * 40, 128), F32))
    else:
        out_spec = pl.BlockSpec((2, 1024, 128), lambda k, *_: (k, 0, 0))
        out_shape = jax.ShapeDtypeStruct((8, 1024, 128), F32)
    return pl.pallas_call(
        functools.partial(ladder_kernel, gc, acc is None, last),
        grid_spec=pltpu.PrefetchScalarGridSpec(
            num_scalar_prefetch=4, grid=(4,), in_specs=ins, out_specs=out_spec, scratch_shapes=scratch
        ),
        out_shape=out_shape,
        compiler_params=pltpu.CompilerParams(vmem_limit_bytes=60 * 2**20),
        cost_estimate=pl.CostEstimate(flops=4 * 64 * 128**3 * gc, bytes_accessed=12 * 10**6, transcendentals=0),
        name="ladder_sum",
    )(*args)


def swap(array, axis):
    return lax.ppermute(array, axis, [(0, 1), (1, 0)])


def shards(densities, amplitudes, partner, qtable, grid_map, coulomb):
    own = (lax.axis_index(KGRP) * 2).astype(jnp.int32).reshape(1)
    across = swap(amplitudes, "zhi")
    dens = densities.reshape(2, 512, G)
    device = lax.axis_index(AXES)
    received, couls, start = [], [], 0
    for q, gc in enumerate(SIZES):
        sent = gather(own, qtable, grid_map, dens, gc, start)
        if q == 0:
            sent, across = lax.optimization_barrier((sent, across))
            here = jnp.stack([amplitudes, across])
            amp = jnp.concatenate([here, swap(here, "core")])
        received.append(lax.all_to_all(sent, AXES, 0, 0, tiled=True))
        couls.append(lax.dynamic_slice(coulomb, (0, start + device * gc), (64, gc)))
        start += 128 * gc
    acc = None
    for q, gc in enumerate(SIZES):
        acc = ladder(own, partner, qtable, couls[q], received[q], amp, acc, q == len(SIZES) - 1, gc)
    away, kept = acc
    both = (kept.astype(F32) + swap(away, "core").astype(F32)).astype(BF)
    parts = lax.all_to_all(both.reshape(64, 64, 128), ("zhi", "band"), 0, 0, tiled=True)
    total = jnp.sum(parts.astype(F32), axis=0) * (1.0 / math.sqrt(G))
    total = total.astype(BF).reshape(2, 8, 4, 4, 32)
    return jnp.transpose(total, (2, 0, 1, 4, 3)).reshape(4, 2, 8, 128)


def solution(mesh):
    split = Mesh(mesh.devices.reshape(2, 2, 32), AXES)
    in_specs = (P(KGRP, "band", None, None), P(KGRP, None, None, None), P(), P(), P(), P())
    out_specs = P("band", KGRP, None, None)
    return jax.shard_map(shards, mesh=split, in_specs=in_specs, out_specs=out_specs, check_vma=False)
```
